256 devices in a mesh: pair: 32 (over z, y), virt: 8 (over x, core).
Axes of the slice: x: 4, y: 4, z: 8, core: 2. Of those that a mesh axis runs over, the one named last changes fastest.
Arguments:
- amplitudes: bfloat16 [16384, 9216], P('pair', 'virt'), may hold values from -6 to 6
- block_mask: int32 [16384, 4], P('pair'), may hold values from 0 to 1, as said below
- integrals: bfloat16 [9216, 9216], P('pair', 'virt'), may hold values from -0.0625 to 0.0625
- mirror: int32 [16384], P('pair'), may hold values from 0 to 16383, as said below
Outputs:
- residual: bfloat16 [16384, 9216], P('pair', 'virt')
The draws below stay inside these ranges and needn't reach their ends.
Inputs may be any that keep to these rules, and one draw needn't show every extreme that they name: mirror is an involution without fixed points; the pair at local row d * 16 + s of pair index p has its mirror on pair index d, at a local row from p * (16) to p * 16 + 512 // 32 - 1. block_mask[g, 2 * t + u] equals block_mask[mirror[g], 2 * u + t]; every pair has at least one active tile pair.
All inputs are finite; a program needn't handle non-finite values.
Results may differ from the reference program's by a relative error of at most 0.0051.
Values may be sent and summed in bfloat16 or wider, within the bound.
No kernel may reach another device: no remote copies, remote signals or barrier semaphores. Data moves between devices by JAX's collectives and lax.ppermute only.
A program may use at most 192 MiB of HBM per device.

```python
import jax
import jax.numpy as jnp

TW = 48
NTILE = 2
PAIR_DEV = 512
V = 96
VV = 9216
NBLK = 4
PAIRS = 16384
N_PAIR = 32


def mirror_table(key):
    key = jax.random.fold_in(key, 11)
    block_rows = PAIR_DEV // N_PAIR
    keys = jax.random.split(key, N_PAIR * N_PAIR + N_PAIR)
    shuffled = jax.vmap(lambda sub: jax.random.permutation(sub, block_rows))(keys[:N_PAIR * N_PAIR])
    shuffled = shuffled.reshape(N_PAIR, N_PAIR, block_rows).astype(jnp.int32)
    inverse = jnp.argsort(shuffled, axis=-1, stable=True).astype(jnp.int32)
    lower = jnp.swapaxes(inverse, 0, 1)
    order = jax.vmap(lambda sub: jax.random.permutation(sub, block_rows))(keys[N_PAIR * N_PAIR:]).astype(jnp.int32)
    evens = order[:, 0::2]
    odds = order[:, 1::2]
    owners = jnp.arange(N_PAIR, dtype=jnp.int32)[:, None]
    matching = jnp.zeros((N_PAIR, block_rows), jnp.int32)
    matching = matching.at[owners, evens].set(odds).at[owners, odds].set(evens)
    source = jnp.arange(N_PAIR, dtype=jnp.int32)[:, None, None]
    target = jnp.arange(N_PAIR, dtype=jnp.int32)[None, :, None]
    within = jnp.where(source < target, shuffled, jnp.where(source > target, lower, matching[:, None, :]))
    return (target * PAIR_DEV + source * block_rows + within).reshape(-1).astype(jnp.int32)


def draw_mirror(key, part):
    return mirror_table(key)


def draw_block_mask(key, part):
    partner = mirror_table(key)
    key = jax.random.fold_in(key, 5)
    key_scores, key_forced = jax.random.split(key)
    index = jnp.arange(PAIRS, dtype=jnp.int32)
    leader = jnp.minimum(index, partner)
    flipped = index > partner
    scores = jax.random.randint(key_scores, (PAIRS, NBLK), 0, 100)
    forced = jax.random.randint(key_forced, (PAIRS,), 0, NBLK)
    owner = leader // PAIR_DEV
    limit = 25 + 60 * owner // max(N_PAIR - 1, 1)
    blocks = jnp.arange(NBLK, dtype=jnp.int32)
    base = ((scores < limit[:, None]) | (blocks[None, :] == forced[:, None])).astype(jnp.int32)
    turned = blocks % NTILE * NTILE + blocks // NTILE
    leading = jnp.take(base, leader, axis=0)
    return jnp.where(flipped[:, None], jnp.take(leading, turned, axis=1), leading).astype(jnp.int32)


def level_of(key, shape, pieces, low, largest):
    def one(axis_at, blocks):
        draws = jax.random.uniform(jax.random.fold_in(jax.random.fold_in(key, 6), axis_at), (blocks,), jnp.float32, low / len(pieces), largest / len(pieces))
        return jnp.repeat(jnp.exp(draws), shape[axis_at] // blocks).reshape((-1,) + (1,) * (len(shape) - axis_at - 1))

    level = one(*pieces[0])
    for cut in pieces[1:]:
        level = level * one(*cut)
    return level


def normal_values(rng, extent, deviation, bound, cuts=(), kind=jnp.bfloat16):
    values = jax.random.normal(rng, extent, jnp.float32) * deviation
    if len(cuts) > 0:
        values = level_of(rng, extent, cuts, -0.22, 0.18) * values
    return jnp.clip(values, min=-bound, max=bound).astype(kind)


def setup_inputs(seed: int = 0) -> dict:
    key_of = jax.random.split(jax.random.key(seed), 5)
    amplitudes = normal_values(key_of[0], (PAIRS, VV), 1.0, 6.0, ((0, 32), (1, 8)))
    block_mask = draw_block_mask(jax.random.fold_in(key_of[4], 71), 0)
    integrals = normal_values(key_of[2], (VV, VV), VV ** -0.5, 0.0625, ((0, 32), (1, 8)))
    mirror = draw_mirror(jax.random.fold_in(key_of[4], 71), 0)
    return {"amplitudes": amplitudes, "block_mask": block_mask, "integrals": integrals, "mirror": mirror}


def reference(amplitudes, block_mask, integrals, mirror):
    column = jnp.arange(VV, dtype=jnp.int32)
    tile_pair = (column // V // TW) * NTILE + (column % V) // TW
    live = jnp.take(block_mask, tile_pair, axis=1) > 0
    masked = jnp.where(live, amplitudes, jnp.zeros_like(amplitudes))
    direct = jnp.dot(masked, integrals, preferred_element_type=jnp.float32).astype(jnp.bfloat16)
    mirrored = jnp.take(direct, mirror, axis=0).reshape(PAIRS, V, V)
    mirrored = jnp.swapaxes(mirrored, 1, 2).reshape(PAIRS, VV)
    total = direct.astype(jnp.float32) + mirrored.astype(jnp.float32)
    return jnp.where(live, total, jnp.zeros_like(total)).astype(jnp.bfloat16)
```

```python
import functools

import jax
import jax.numpy as jnp
from jax import lax
from jax.experimental import pallas as pl
from jax.experimental.pallas import tpu as pltpu
from jax.sharding import Mesh, PartitionSpec as P

TW = 48
V = 96
Z, Y, X, C = 8, 4, 4, 2
VIRT = X * C
PAIR = Z * Y
A_BLOCK = V // VIRT
ROWS = 512
WIDTH = A_BLOCK * V
DEPTH = 288
SLOT = ROWS // PAIR
PIECE = A_BLOCK * A_BLOCK


def shift(axis, by):
    n = {"z": Z, "y": Y, "x": X, "c": C}[axis]
    return [(i, (i + by) % n) for i in range(n)]


def product_kernel(where_ref, *refs):
    blocks, b_ref, o_ref, a_ref = refs[:VIRT], refs[VIRT], refs[VIRT + 1], refs[VIRT + 2]
    for k, block in enumerate(blocks):
        at = pl.multiple_of(where_ref[k] * DEPTH, 16)
        a_ref[pl.ds(at, DEPTH), :] = block[0]
    o_ref[0] = lax.dot_general(
        a_ref[...], b_ref[...], (((0,), (0,)), ((), ())), preferred_element_type=jnp.float32
    ).astype(o_ref.dtype)


def product(where, blocks, b):
    groups, depth, rows = blocks[0].shape
    step = 256
    parts = rows // step
    a_spec = pl.BlockSpec((1, depth, step), lambda i, w: (i // parts, 0, i % parts))
    return pl.pallas_call(
        product_kernel,
        grid_spec=pltpu.PrefetchScalarGridSpec(
            num_scalar_prefetch=1,
            grid=(groups * parts,),
            in_specs=[a_spec] * VIRT + [pl.BlockSpec((VIRT * depth, WIDTH), lambda i, w: (0, 0))],
            out_specs=pl.BlockSpec((1, step, WIDTH), lambda i, w: (i // parts, i % parts, 0)),
            scratch_shapes=[pltpu.VMEM((VIRT * depth, step), jnp.bfloat16)],
        ),
        out_shape=jax.ShapeDtypeStruct((groups, rows, WIDTH), jnp.bfloat16),
        compiler_params=pltpu.CompilerParams(vmem_limit_bytes=48 * 2**20),
    )(where, *blocks, b)


def gather_x(block):
    half = block.shape[0] // 2
    left = lax.ppermute(block, "x", shift("x", 1))
    right = lax.ppermute(block, "x", shift("x", -1))
    far_low = lax.ppermute(left[:half], "x", shift("x", 1))
    far_high = lax.ppermute(right[half:], "x", shift("x", -1))
    return [block, left, right, jnp.concatenate([far_low, far_high], axis=0)]


def local(amplitudes, block_mask, integrals, mirror):
    z, y, x, c = (lax.axis_index(n) for n in "zyxc")
    virt = x * C + c
    pair = z * Y + y
    tile = virt * A_BLOCK // TW
    active = lax.dynamic_slice(block_mask, (0, 2 * tile), (ROWS, 2)) > 0
    column = jnp.arange(WIDTH, dtype=jnp.int32)
    first = (column % V) < TW
    live = jnp.where(first[None, :], active[:, :1], active[:, 1:])

    whole = lax.all_gather(integrals, "z", axis=0, tiled=True)

    masked = jnp.where(live, amplitudes, jnp.zeros_like(amplitudes))
    turned = masked.T.reshape(Y, DEPTH, ROWS)
    mine = lax.all_to_all(turned, "y", split_axis=0, concat_axis=0, tiled=True)
    along = gather_x(mine)
    across = [lax.ppermute(b, "c", shift("c", 1)) for b in along]
    order = [(x + d) % X for d in (0, -1, 1, 2)]
    where = jnp.stack([o * C + c for o in order] + [o * C + 1 - c for o in order]).astype(jnp.int32)
    partial = product(where, along + across, whole)

    direct = lax.psum_scatter(partial, "y", scatter_dimension=0, tiled=False)

    received = lax.all_to_all(direct.reshape(PAIR, SLOT, WIDTH), ("z", "y"), split_axis=0, concat_axis=0, tiled=True)
    received = received.reshape(ROWS, WIDTH)
    position = mirror // ROWS * SLOT + mirror % ROWS - pair * SLOT
    row = jnp.arange(ROWS, dtype=jnp.int32)
    pick = (position[:, None] == row[None, :]).astype(jnp.bfloat16)
    picked = jnp.dot(pick, received, preferred_element_type=jnp.float32).astype(jnp.bfloat16)
    outer, middle, inner = column // PIECE, column % PIECE // A_BLOCK, column % A_BLOCK
    send = ((inner * V + outer * A_BLOCK + middle)[:, None] == column[None, :]).astype(jnp.bfloat16)
    split = lax.dot_general(
        send, picked, (((1,), (1,)), ((), ())), preferred_element_type=jnp.float32
    ).astype(jnp.bfloat16)
    swapped = lax.all_to_all(split.reshape(VIRT, PIECE, ROWS), ("x", "c"), split_axis=0, concat_axis=0, tiled=True)
    swapped = swapped.reshape(WIDTH, ROWS)
    land = ((middle * V + outer * A_BLOCK + inner)[:, None] == column[None, :]).astype(jnp.bfloat16)
    mirrored = lax.dot_general(swapped, land, (((0,), (0,)), ((), ())), preferred_element_type=jnp.float32)
    total = direct.astype(jnp.float32) + mirrored
    return jnp.where(live, total, jnp.zeros_like(total)).astype(jnp.bfloat16)


def solution(mesh):
    grid = Mesh(mesh.devices.reshape(Z, Y, X, C), ("z", "y", "x", "c"))
    rows, columns = ("z", "y"), ("x", "c")
    in_specs = (P(rows, columns), P(rows, None), P(rows, columns), P(rows))
    return jax.shard_map(local, mesh=grid, in_specs=in_specs, out_specs=P(rows, columns), check_vma=False)
```

```python
import jax
import jax.numpy as jnp
from jax import lax
from jax.experimental import pallas as pl
from jax.experimental.pallas import tpu as pltpu
from jax.sharding import Mesh, PartitionSpec as P

TW = 48
V = 96
SIZE = {"z": 8, "y": 4, "x": 4, "c": 2}
NZ, NY, NX = 8, 4, 4
VIRT = 8
PAIR = 32
A_BLOCK = V // VIRT
ROWS = 512
WIDTH = A_BLOCK * V
DEPTH = 288
SLOT = ROWS // PAIR
PLANE = NZ * SLOT
PIECE = A_BLOCK * A_BLOCK
HALF = ROWS // 2
F32 = jnp.float32
BF16 = jnp.bfloat16
ROOM = pltpu.CompilerParams(vmem_limit_bytes=48 * 2**20)


def after(value, *others):
    return lax.optimization_barrier((value, *others))[0]


def move(array, axis, by):
    n = SIZE[axis]
    return lax.ppermute(array, axis, [(i, (i + by) % n) for i in range(n)])


def product_kernel(outs_of, where_ref, *refs):
    blocks, b_ref, outs, a_ref = refs[:VIRT + 2], refs[VIRT + 2], refs[VIRT + 3:-1], refs[-1]
    for k, block in enumerate(blocks):
        at = pl.multiple_of(where_ref[k - 2 if k >= VIRT else k] * DEPTH, 16)
        for r in range(block.shape[0]):
            group = r + NY // 2 if k >= VIRT else r
            lane = pl.multiple_of(where_ref[VIRT + group] * PLANE, PLANE)
            a_ref[pl.ds(at, DEPTH), pl.ds(lane, PLANE)] = block[r]
    value = lax.dot_general(a_ref[...], b_ref[...], (((0,), (0,)), ((), ())), preferred_element_type=F32)
    for g in range(len(outs) // outs_of):
        @pl.when(pl.program_id(0) == g)
        def _():
            rows = ROWS // outs_of
            for h in range(outs_of):
                out = outs[g * outs_of + h]
                out[...] = value[h * rows:(h + 1) * rows, :].astype(out.dtype)


def product(where, slots, blocks, b, outs_of, kind):
    at = VIRT + NY
    shape = (ROWS // outs_of, WIDTH)

    def spec(groups):
        return pl.BlockSpec((groups, DEPTH, PLANE), lambda g, w: (0, 0, w[at + g]))

    def kernel(*refs):
        product_kernel(outs_of, *refs)

    return pl.pallas_call(
        kernel,
        grid_spec=pltpu.PrefetchScalarGridSpec(
            num_scalar_prefetch=1,
            grid=(len(slots),),
            in_specs=[spec(NY)] * (VIRT - 2) + [spec(NY // 2)] * 4 + [pl.BlockSpec((VIRT * DEPTH, WIDTH), lambda g, w: (0, 0))],
            out_specs=[pl.BlockSpec(shape, lambda g, w: (0, 0))] * (len(slots) * outs_of),
            scratch_shapes=[pltpu.VMEM((VIRT * DEPTH, ROWS), BF16)],
        ),
        out_shape=[jax.ShapeDtypeStruct(shape, kind)] * (len(slots) * outs_of),
        compiler_params=ROOM,
    )(jnp.stack(where + slots).astype(jnp.int32), *blocks, b)


def gather_x(block):
    half = NY // 2
    left = move(block, "x", 1)
    right = move(block, "x", -1)
    far_low = move(left[:half], "x", 1)
    far_high = move(right[half:], "x", -1)
    return [b for one in (block, left, right, far_low, far_high) for b in (one, move(one, "c", 1))]


def joined(near, far):
    return (near.astype(F32) + far.astype(F32)).astype(BF16)


def deal_kernel(here_ref, own_ref, *refs):
    got, refs, direct_ref = refs[:4], refs[4:-1], refs[-1]
    for h in range(2):
        rows = slice(h * HALF, (h + 1) * HALF)
        direct_ref[rows, :] = (own_ref[rows, :] + got[h][...].astype(F32) + got[2 + h][...].astype(F32)).astype(BF16)
    for d in range(NZ):
        target = lax.rem(here_ref[0] + d, NZ)
        for y in range(NY):
            at = pl.multiple_of(y * PLANE + target * SLOT, SLOT)
            refs[d][y * SLOT:(y + 1) * SLOT, :] = direct_ref[pl.ds(at, SLOT), :]
    for y in range(NY):
        refs[NZ][y] = direct_ref[y * PLANE:(y + 1) * PLANE, :]


def deal(here, own, *got):
    shapes = [(NY * SLOT, WIDTH)] * NZ + [(NY, PLANE, WIDTH)]
    vmem = pl.BlockSpec(memory_space=pltpu.VMEM)
    return pl.pallas_call(
        deal_kernel,
        in_specs=[pl.BlockSpec(memory_space=pltpu.SMEM)] + [vmem] * 5,
        out_specs=[vmem] * (NZ + 1),
        out_shape=[jax.ShapeDtypeStruct(s, BF16) for s in shapes],
        scratch_shapes=[pltpu.VMEM((ROWS, WIDTH), BF16)],
        compiler_params=ROOM,
    )(here, own, *got)


def turn_kernel(pick_ref, send_ref, *refs):
    pieces, outs, x_ref = refs[:NZ], refs[NZ:-1], refs[-1]
    step = NY * SLOT
    for d, piece in enumerate(pieces):
        x_ref[d * step:(d + 1) * step, :] = piece[...]
    picked = jnp.dot(pick_ref[...], x_ref[...], preferred_element_type=F32).astype(BF16)
    turned = lax.dot_general(send_ref[...], picked, (((1,), (1,)), ((), ())), preferred_element_type=F32).astype(BF16)
    for d, out in enumerate(outs):
        for core in range(2):
            out[core] = turned[(2 * d + core) * PIECE:(2 * d + core + 1) * PIECE, :]


def turn(pick, send, pieces):
    vmem = pl.BlockSpec(memory_space=pltpu.VMEM)
    return pl.pallas_call(
        turn_kernel,
        in_specs=[vmem] * (2 + NZ),
        out_specs=[vmem] * NX,
        out_shape=[jax.ShapeDtypeStruct((2, PIECE, ROWS), BF16)] * NX,
        scratch_shapes=[pltpu.VMEM((ROWS, WIDTH), BF16)],
        compiler_params=ROOM,
    )(pick, send, *pieces)


def finish_kernel(active_ref, land_ref, *refs):
    blocks, across, home, o_ref, u_ref, d_ref = refs[:NX], *refs[NX:]
    for k, block in enumerate(blocks):
        u_ref[2 * k * PIECE:(2 * k + 1) * PIECE, :] = block[0]
        u_ref[(2 * k + 1) * PIECE:(2 * k + 2) * PIECE, :] = across[k]
    for y in range(NY):
        for z in range(NZ):
            at = (z * NY + y) * SLOT
            d_ref[at:at + SLOT, :] = home[y, z * SLOT:(z + 1) * SLOT, :]
    mirrored = lax.dot_general(u_ref[...], land_ref[...], (((0,), (0,)), ((), ())), preferred_element_type=F32)
    total = d_ref[...].astype(F32) + mirrored
    column = lax.broadcasted_iota(jnp.int32, (ROWS, WIDTH), 1)
    live = jnp.where(lax.rem(column, V) < TW, active_ref[:, :1], active_ref[:, 1:]) > 0
    o_ref[...] = jnp.where(live, total, 0).astype(BF16)


def finish(active, land, blocks, across, home):
    vmem = pl.BlockSpec(memory_space=pltpu.VMEM)
    return pl.pallas_call(
        finish_kernel,
        in_specs=[vmem] * (4 + NX),
        out_specs=vmem,
        out_shape=jax.ShapeDtypeStruct((ROWS, WIDTH), BF16),
        scratch_shapes=[pltpu.VMEM((WIDTH, ROWS), BF16), pltpu.VMEM((ROWS, WIDTH), BF16)],
        compiler_params=ROOM,
    )(active, land, *blocks, across, home)


def local(amplitudes, block_mask, integrals, mirror):
    z, y, x, c = (lax.axis_index(n) for n in "zyxc")
    pair = z * NY + y
    tile = (x * 2 + c) * A_BLOCK // TW
    here = jnp.stack([z]).astype(jnp.int32)
    active = lax.dynamic_slice(block_mask, (0, 2 * tile), (ROWS, 2))
    column = jnp.arange(WIDTH, dtype=jnp.int32)
    live = jnp.where(((column % V) < TW)[None, :], active[:, :1], active[:, 1:]) > 0

    whole = lax.all_gather(integrals, "z", axis=0, tiled=True)

    masked = jnp.where(live, amplitudes, jnp.zeros_like(amplitudes))
    masked = jnp.swapaxes(masked.reshape(NZ, NY, SLOT, WIDTH), 0, 1).reshape(ROWS, WIDTH)
    turned = masked.T.reshape(NY, DEPTH, ROWS)

    def toward(d):
        return lax.dynamic_slice_in_dim(turned, (y + d) % NY, 1, axis=0)

    groups = [toward(0), move(toward(2), "y", 2), move(toward(-1), "y", -1), move(toward(1), "y", 1)]
    blocks = gather_x(jnp.concatenate(groups, axis=0))
    where = [(x + d) % NX * 2 + core for d in (0, -1, 1, 2) for core in (c, 1 - c)]
    where = where + [(y + d) % NY for d in (0, 2, 1, -1)]
    far_slot, up_slot, down_slot = ((y + d) % NY for d in (2, 1, -1))

    far_low, far_high = product(where, [far_slot], blocks, whole, 2, BF16)
    from_down = move(far_low, "y", 1)
    from_up = move(far_high, "y", -1)
    up_low, up_high, down_low, down_high = product(where, [up_slot, down_slot], blocks, after(whole, far_low), 2, BF16)
    from_down_high = move(up_high, "y", 1)
    from_up_low = move(down_low, "y", -1)
    up_low, down_high = joined(up_low, from_down), joined(down_high, from_up)
    from_down_low = move(up_low, "y", 1)
    from_up_high = move(down_high, "y", -1)
    own, = product(where, [y], blocks, after(whole, up_low, down_high), 1, F32)
    dealt = deal(here, own, from_down_low, from_down_high, from_up_low, from_up_high)

    pieces = {d: move(dealt[d], "z", d) for d in (4, 3, 5, 2, 6, 1, 7)}
    pieces = [dealt[0]] + [pieces[d] for d in range(1, NZ)]
    home = lax.all_to_all(dealt[NZ], "y", split_axis=0, concat_axis=0, tiled=True)

    source = mirror // ROWS
    position = (z + NZ - source // NY) % NZ * (NY * SLOT) + source % NY * SLOT + mirror % ROWS - pair * SLOT
    row = jnp.arange(ROWS, dtype=jnp.int32)
    pick = (position[:, None] == row[None, :]).astype(BF16)
    core, step, second, first = column // PIECE % 2, column // (2 * PIECE), column % PIECE // A_BLOCK, column % A_BLOCK
    target = (x + step) % NX * 2 + (c + core) % 2
    send = ((first * V + target * A_BLOCK + second)[:, None] == column[None, :]).astype(BF16)
    origin = (x + NX - step) % NX * 2 + (c + core) % 2
    land = ((second * V + origin * A_BLOCK + first)[:, None] == column[None, :]).astype(BF16)

    sent = turn(pick, send, pieces)
    arrived = [sent[0]] + [move(sent[d], "x", d) for d in range(1, NX)]
    across = move(jnp.concatenate([block[1:] for block in arrived], axis=0), "c", 1)
    return finish(active, land, arrived, across, home)


def solution(mesh):
    grid = Mesh(mesh.devices.reshape(tuple(SIZE.values())), tuple(SIZE))
    rows, columns = ("z", "y"), ("x", "c")
    in_specs = (P(rows, columns), P(rows, None), P(rows, columns), P(rows))
    return jax.shard_map(local, mesh=grid, in_specs=in_specs, out_specs=P(rows, columns), check_vma=False)
```

```python
import jax
import jax.numpy as jnp
from jax import lax
from jax.experimental import pallas as pl
from jax.experimental.pallas import tpu as pltpu
from jax.sharding import Mesh, PartitionSpec as P

TW = 48
V = 96
SIZE = {"z": 8, "y": 4, "x": 4, "c": 2}
NZ, NY, NX = 8, 4, 4
VIRT = 8
PAIR = 32
A_BLOCK = V // VIRT
ROWS = 512
WIDTH = A_BLOCK * V
DEPTH = 288
SLOT = ROWS // PAIR
PLANE = NZ * SLOT
PIECE = A_BLOCK * A_BLOCK
HALF = ROWS // 2
F32 = jnp.float32
BF16 = jnp.bfloat16
ROOM = pltpu.CompilerParams(vmem_limit_bytes=48 * 2**20)


def move(array, axis, by):
    n = SIZE[axis]
    return lax.ppermute(array, axis, [(i, (i + by) % n) for i in range(n)])


def product_kernel(outs_of, where_ref, *refs):
    blocks, b_ref, outs, a_ref = refs[:VIRT], refs[VIRT], refs[VIRT + 1:-1], refs[-1]
    for k, block in enumerate(blocks):
        a_ref[pl.ds(pl.multiple_of(where_ref[k] * DEPTH, 16), DEPTH), :] = block[0]
    value = lax.dot_general(a_ref[...], b_ref[...], (((0,), (0,)), ((), ())), preferred_element_type=F32)
    for g in range(len(outs) // outs_of):
        @pl.when(pl.program_id(0) == g)
        def _():
            rows = ROWS // outs_of
            for h in range(outs_of):
                out = outs[g * outs_of + h]
                out[...] = value[h * rows:(h + 1) * rows, :].astype(out.dtype)


def product(where, group, count, blocks, b, outs_of, kind, *first):
    shape = (ROWS // outs_of, WIDTH)
    whole = pl.BlockSpec((1, DEPTH, ROWS), lambda g, w: (group + g, 0, 0))
    part = pl.BlockSpec((1, DEPTH, ROWS), lambda g, w: (group % (NY // 2) + g, 0, 0))

    def kernel(*refs):
        product_kernel(outs_of, *refs[:VIRT + 2], *refs[VIRT + 2 + len(first):])

    return pl.pallas_call(
        kernel,
        grid_spec=pltpu.PrefetchScalarGridSpec(
            num_scalar_prefetch=1,
            grid=(count,),
            in_specs=[whole] * (VIRT - 2) + [part] * 2 + [pl.BlockSpec((VIRT * DEPTH, WIDTH), lambda g, w: (0, 0))]
            + [pl.BlockSpec(memory_space=pl.ANY)] * len(first),
            out_specs=[pl.BlockSpec(shape, lambda g, w: (0, 0))] * (count * outs_of),
            scratch_shapes=[pltpu.VMEM((VIRT * DEPTH, ROWS), BF16)],
        ),
        out_shape=[jax.ShapeDtypeStruct(shape, kind)] * (count * outs_of),
        compiler_params=ROOM,
    )(where, *blocks, b, *first)


def gather_x(block):
    half = NY // 2
    left = move(block, "x", 1)
    right = move(block, "x", -1)
    far_low = move(left[:half], "x", 1)
    far_high = move(right[half:], "x", -1)
    return [b for one in (block, left, right, far_low, far_high) for b in (one, move(one, "c", 1))]


def joined(near, far):
    return (near.astype(F32) + far.astype(F32)).astype(BF16)


def total_kernel(own_ref, *refs):
    got, out_ref = refs[:4], refs[4]
    for h in range(2):
        rows = slice(h * HALF, (h + 1) * HALF)
        out_ref[rows, :] = (own_ref[rows, :] + got[h][...].astype(F32) + got[2 + h][...].astype(F32)).astype(BF16)


def total(own, *got):
    vmem = pl.BlockSpec(memory_space=pltpu.VMEM)
    return pl.pallas_call(
        total_kernel,
        in_specs=[vmem] * 5,
        out_specs=vmem,
        out_shape=jax.ShapeDtypeStruct((ROWS, WIDTH), BF16),
        compiler_params=ROOM,
    )(own, *got)


def turn_kernel(pick_ref, send_ref, received_ref, *outs):
    picked = jnp.dot(pick_ref[...], received_ref[...], preferred_element_type=F32).astype(BF16)
    turned = lax.dot_general(send_ref[...], picked, (((1,), (1,)), ((), ())), preferred_element_type=F32).astype(BF16)
    for d, out in enumerate(outs):
        for core in range(2):
            out[core] = turned[(2 * d + core) * PIECE:(2 * d + core + 1) * PIECE, :]


def turn(pick, send, received):
    vmem = pl.BlockSpec(memory_space=pltpu.VMEM)
    return pl.pallas_call(
        turn_kernel,
        in_specs=[vmem] * 3,
        out_specs=[vmem] * NX,
        out_shape=[jax.ShapeDtypeStruct((2, PIECE, ROWS), BF16)] * NX,
        compiler_params=ROOM,
    )(pick, send, received)


def finish_kernel(active_ref, land_ref, direct_ref, *refs):
    blocks, across, o_ref, u_ref = refs[:NX], *refs[NX:]
    for k, block in enumerate(blocks):
        u_ref[2 * k * PIECE:(2 * k + 1) * PIECE, :] = block[0]
        u_ref[(2 * k + 1) * PIECE:(2 * k + 2) * PIECE, :] = across[k]
    mirrored = lax.dot_general(u_ref[...], land_ref[...], (((0,), (0,)), ((), ())), preferred_element_type=F32)
    value = direct_ref[...].astype(F32) + mirrored
    column = lax.broadcasted_iota(jnp.int32, (ROWS, WIDTH), 1)
    live = jnp.where(lax.rem(column, V) < TW, active_ref[:, :1], active_ref[:, 1:]) > 0
    o_ref[...] = jnp.where(live, value, 0).astype(BF16)


def finish(active, land, direct, blocks, across):
    vmem = pl.BlockSpec(memory_space=pltpu.VMEM)
    return pl.pallas_call(
        finish_kernel,
        in_specs=[vmem] * (4 + NX),
        out_specs=vmem,
        out_shape=jax.ShapeDtypeStruct((ROWS, WIDTH), BF16),
        scratch_shapes=[pltpu.VMEM((WIDTH, ROWS), BF16)],
        compiler_params=ROOM,
    )(active, land, direct, *blocks, across)


def local(amplitudes, block_mask, integrals, mirror):
    z, y, x, c = (lax.axis_index(n) for n in "zyxc")
    pair = z * NY + y
    tile = (x * 2 + c) * A_BLOCK // TW
    active = lax.dynamic_slice(block_mask, (0, 2 * tile), (ROWS, 2))
    column = jnp.arange(WIDTH, dtype=jnp.int32)
    live = jnp.where(((column % V) < TW)[None, :], active[:, :1], active[:, 1:]) > 0

    whole = lax.all_gather(integrals, "z", axis=0, tiled=True)

    masked = jnp.where(live, amplitudes, jnp.zeros_like(amplitudes))
    turned = masked.T.reshape(NY, DEPTH, ROWS)

    def toward(d):
        return lax.dynamic_slice_in_dim(turned, (y + d) % NY, 1, axis=0)

    groups = [toward(0), move(toward(2), "y", 2), move(toward(-1), "y", -1), move(toward(1), "y", 1)]
    blocks = gather_x(jnp.concatenate(groups, axis=0))
    low, high = blocks[:VIRT], blocks[:VIRT - 2] + blocks[VIRT:]
    where = jnp.stack([(x + d) % NX * 2 + core for d in (0, -1, 1, 2) for core in (c, 1 - c)]).astype(jnp.int32)

    far_low, far_high = product(where, 1, 1, low, whole, 2, BF16)
    from_down = move(far_low, "y", 1)
    from_up = move(far_high, "y", -1)
    up_low, up_high, down_low, down_high = product(where, 2, 2, high, whole, 2, BF16, far_low)
    from_down_high = move(up_high, "y", 1)
    from_up_low = move(down_low, "y", -1)
    up_low, down_high = joined(up_low, from_down), joined(down_high, from_up)
    from_down_low = move(up_low, "y", 1)
    from_up_high = move(down_high, "y", -1)
    own, = product(where, 0, 1, low, whole, 1, F32, up_low, down_high)
    direct = total(own, from_down_low, from_down_high, from_up_low, from_up_high)

    source = mirror // ROWS
    position = source * SLOT + mirror % ROWS - pair * SLOT
    row = jnp.arange(ROWS, dtype=jnp.int32)
    pick = (position[:, None] == row[None, :]).astype(BF16)
    core, step, second, first = column // PIECE % 2, column // (2 * PIECE), column % PIECE // A_BLOCK, column % A_BLOCK
    target = (x + step) % NX * 2 + (c + core) % 2
    send = ((first * V + target * A_BLOCK + second)[:, None] == column[None, :]).astype(BF16)
    origin = (x + NX - step) % NX * 2 + (c + core) % 2
    land = ((second * V + origin * A_BLOCK + first)[:, None] == column[None, :]).astype(BF16)

    received = lax.all_to_all(direct.reshape(PAIR, SLOT, WIDTH), ("z", "y"), split_axis=0, concat_axis=0, tiled=True)
    sent = turn(pick, send, received.reshape(ROWS, WIDTH))
    arrived = [sent[0]] + [move(sent[d], "x", d) for d in range(1, NX)]
    across = move(jnp.concatenate([block[1:] for block in arrived], axis=0), "c", 1)
    return finish(active, land, direct, arrived, across)


def solution(mesh):
    grid = Mesh(mesh.devices.reshape(tuple(SIZE.values())), tuple(SIZE))
    rows, columns = ("z", "y"), ("x", "c")
    in_specs = (P(rows, columns), P(rows, None), P(rows, columns), P(rows))
    return jax.shard_map(local, mesh=grid, in_specs=in_specs, out_specs=P(rows, columns), check_vma=False)
```

```python
import jax
import jax.numpy as jnp
from jax import lax
from jax.experimental import pallas as pl
from jax.experimental.pallas import tpu as pltpu
from jax.sharding import Mesh, PartitionSpec as P

TW = 48
V = 96
SIZE = {"z": 8, "y": 4, "x": 4, "c": 2}
NZ, NY, NX = 8, 4, 4
VIRT = 8
PAIR = 32
A_BLOCK = V // VIRT
ROWS = 512
WIDTH = A_BLOCK * V
DEPTH = 288
SLOT = ROWS // PAIR
PLANE = NZ * SLOT
PIECE = A_BLOCK * A_BLOCK
HALF = ROWS // 2
CHUNKS = ((0, 8), (8, 4))
F32 = jnp.float32
BF16 = jnp.bfloat16
ROOM = pltpu.CompilerParams(vmem_limit_bytes=48 * 2**20)


def move(array, axis, by):
    n = SIZE[axis]
    return lax.ppermute(array, axis, [(i, (i + by) % n) for i in range(n)])


def product_kernel(outs_of, where_ref, *refs):
    blocks, b_ref, outs, a_ref = refs[:VIRT], refs[VIRT], refs[VIRT + 1:-1], refs[-1]
    for k, block in enumerate(blocks):
        a_ref[pl.ds(pl.multiple_of(where_ref[k] * DEPTH, 16), DEPTH), :] = block[0]
    value = lax.dot_general(a_ref[...], b_ref[...], (((0,), (0,)), ((), ())), preferred_element_type=F32)
    for g in range(len(outs) // outs_of):
        @pl.when(pl.program_id(0) == g)
        def _():
            rows = ROWS // outs_of
            for h in range(outs_of):
                out = outs[g * outs_of + h]
                out[...] = value[h * rows:(h + 1) * rows, :].astype(out.dtype)


def product(where, group, count, blocks, b, outs_of, kind, *first):
    shape = (ROWS // outs_of, WIDTH)
    whole = pl.BlockSpec((1, DEPTH, ROWS), lambda g, w: (group + g, 0, 0))
    part = pl.BlockSpec((1, DEPTH, ROWS), lambda g, w: (group % (NY // 2) + g, 0, 0))

    def kernel(*refs):
        product_kernel(outs_of, *refs[:VIRT + 2], *refs[VIRT + 2 + len(first):])

    return pl.pallas_call(
        kernel,
        grid_spec=pltpu.PrefetchScalarGridSpec(
            num_scalar_prefetch=1,
            grid=(count,),
            in_specs=[whole] * (VIRT - 2) + [part] * 2 + [pl.BlockSpec((VIRT * DEPTH, WIDTH), lambda g, w: (0, 0))]
            + [pl.BlockSpec(memory_space=pl.ANY)] * len(first),
            out_specs=[pl.BlockSpec(shape, lambda g, w: (0, 0))] * (count * outs_of),
            scratch_shapes=[pltpu.VMEM((VIRT * DEPTH, ROWS), BF16)],
        ),
        out_shape=[jax.ShapeDtypeStruct(shape, kind)] * (count * outs_of),
        compiler_params=ROOM,
    )(where, *blocks, b, *first)


def gather_x(block):
    half = NY // 2
    left = move(block, "x", 1)
    right = move(block, "x", -1)
    far_low = move(left[:half], "x", 1)
    far_high = move(right[half:], "x", -1)
    return [b for one in (block, left, right, far_low, far_high) for b in (one, move(one, "c", 1))]


def joined(near, far):
    return (near.astype(F32) + far.astype(F32)).astype(BF16)


def total_kernel(own_ref, *refs):
    got, outs = refs[:4], refs[4:]
    for h in range(2):
        rows = slice(h * HALF, (h + 1) * HALF)
        value = (own_ref[rows, :] + got[h][...].astype(F32) + got[2 + h][...].astype(F32)).astype(BF16)
        for (first, count), out in zip(CHUNKS, outs):
            out[rows, :] = value[:, first * V:(first + count) * V]


def total(own, *got):
    vmem = pl.BlockSpec(memory_space=pltpu.VMEM)
    return pl.pallas_call(
        total_kernel,
        in_specs=[vmem] * 5,
        out_specs=[vmem] * len(CHUNKS),
        out_shape=[jax.ShapeDtypeStruct((ROWS, count * V), BF16) for _, count in CHUNKS],
        compiler_params=ROOM,
    )(own, *got)


def turn_kernel(send_ref, *refs):
    outs, rows = refs[-NX:], refs[0][...]
    if len(refs) == NX + 2:
        rows = jnp.dot(refs[1][...], rows, preferred_element_type=F32).astype(BF16)
    turned = lax.dot_general(send_ref[...], rows, (((1,), (1,)), ((), ())), preferred_element_type=F32).astype(BF16)
    size = turned.shape[0] // VIRT
    for d, out in enumerate(outs):
        for core in range(2):
            out[core] = turned[(2 * d + core) * size:(2 * d + core + 1) * size, :]


def turn(send, rows, *pick):
    vmem = pl.BlockSpec(memory_space=pltpu.VMEM)
    return pl.pallas_call(
        turn_kernel,
        in_specs=[vmem] * (2 + len(pick)),
        out_specs=[vmem] * NX,
        out_shape=[jax.ShapeDtypeStruct((2, send.shape[0] // VIRT, ROWS), BF16)] * NX,
        compiler_params=ROOM,
    )(send, rows, *pick)


def swap(sent):
    arrived = [sent[0]] + [move(sent[d], "x", d) for d in range(1, NX)]
    return arrived + [move(jnp.concatenate([block[1:] for block in arrived], axis=0), "c", 1)]


def stacked(blocks, u_ref):
    size = u_ref.shape[0] // VIRT
    for k in range(NX):
        u_ref[2 * k * size:(2 * k + 1) * size, :] = blocks[k][0]
        u_ref[(2 * k + 1) * size:(2 * k + 2) * size, :] = blocks[NX][k]


def back_kernel(*refs):
    stacked(refs[:NX + 1], refs[-1])
    refs[NX + 1][...] = refs[-1][...].T


def back(blocks):
    vmem = pl.BlockSpec(memory_space=pltpu.VMEM)
    width = VIRT * blocks[0].shape[1]
    return pl.pallas_call(
        back_kernel,
        in_specs=[vmem] * (1 + NX),
        out_specs=vmem,
        out_shape=jax.ShapeDtypeStruct((ROWS, width), BF16),
        scratch_shapes=[pltpu.VMEM((width, ROWS), BF16)],
        compiler_params=ROOM,
    )(*blocks)


def begin_kernel(land_ref, *refs):
    blocks, direct, o_ref, u_ref = refs[:NX + 1], refs[NX + 1:-2], refs[-2], refs[-1]
    stacked(blocks, u_ref)
    o_ref[...] = lax.dot_general(u_ref[...], land_ref[...], (((0,), (0,)), ((), ())), preferred_element_type=F32)
    for (first, count), part in zip(CHUNKS, direct):
        at = slice(first * V, (first + count) * V)
        o_ref[:, at] = o_ref[:, at] + part[...].astype(F32)


def begin(land, blocks, direct):
    vmem = pl.BlockSpec(memory_space=pltpu.VMEM)
    return pl.pallas_call(
        begin_kernel,
        in_specs=[vmem] * (2 + NX + len(direct)),
        out_specs=vmem,
        out_shape=jax.ShapeDtypeStruct((ROWS, WIDTH), F32),
        scratch_shapes=[pltpu.VMEM((land.shape[0], ROWS), BF16)],
        compiler_params=ROOM,
    )(land, *blocks, *direct)


def finish_kernel(active_ref, begun_ref, pick_ref, land_ref, received_ref, o_ref):
    picked = jnp.dot(pick_ref[...], received_ref[...], preferred_element_type=F32).astype(BF16)
    value = begun_ref[...] + jnp.dot(picked, land_ref[...], preferred_element_type=F32)
    column = lax.broadcasted_iota(jnp.int32, (ROWS, WIDTH), 1)
    live = jnp.where(lax.rem(column, V) < TW, active_ref[:, :1], active_ref[:, 1:]) > 0
    o_ref[...] = jnp.where(live, value, 0).astype(BF16)


def finish(active, begun, pick, land, received):
    vmem = pl.BlockSpec(memory_space=pltpu.VMEM)
    return pl.pallas_call(
        finish_kernel,
        in_specs=[vmem] * 5,
        out_specs=vmem,
        out_shape=jax.ShapeDtypeStruct((ROWS, WIDTH), BF16),
        compiler_params=ROOM,
    )(active, begun, pick, land, received)


def over_pair(rows):
    width = rows.shape[1]
    moved = lax.all_to_all(rows.reshape(PAIR, SLOT, width), ("z", "y"), split_axis=0, concat_axis=0, tiled=True)
    return moved.reshape(ROWS, width)


def local(amplitudes, block_mask, integrals, mirror):
    z, y, x, c = (lax.axis_index(n) for n in "zyxc")
    pair = z * NY + y
    tile = (x * 2 + c) * A_BLOCK // TW
    active = lax.dynamic_slice(block_mask, (0, 2 * tile), (ROWS, 2))
    column = jnp.arange(WIDTH, dtype=jnp.int32)
    live = jnp.where(((column % V) < TW)[None, :], active[:, :1], active[:, 1:]) > 0

    whole = lax.all_gather(integrals, "z", axis=0, tiled=True)

    masked = jnp.where(live, amplitudes, jnp.zeros_like(amplitudes))
    turned = masked.T.reshape(NY, DEPTH, ROWS)

    def toward(d):
        return lax.dynamic_slice_in_dim(turned, (y + d) % NY, 1, axis=0)

    groups = [toward(0), move(toward(2), "y", 2), move(toward(-1), "y", -1), move(toward(1), "y", 1)]
    blocks = gather_x(jnp.concatenate(groups, axis=0))
    low, high = blocks[:VIRT], blocks[:VIRT - 2] + blocks[VIRT:]
    where = jnp.stack([(x + d) % NX * 2 + core for d in (0, -1, 1, 2) for core in (c, 1 - c)]).astype(jnp.int32)

    far_low, far_high = product(where, 1, 1, low, whole, 2, BF16)
    from_down = move(far_low, "y", 1)
    from_up = move(far_high, "y", -1)
    up_low, up_high, down_low, down_high = product(where, 2, 2, high, whole, 2, BF16, far_low)
    from_down_high = move(up_high, "y", 1)
    from_up_low = move(down_low, "y", -1)
    up_low, down_high = joined(up_low, from_down), joined(down_high, from_up)
    from_down_low = move(up_low, "y", 1)
    from_up_high = move(down_high, "y", -1)
    own, = product(where, 0, 1, low, whole, 1, F32, up_low, down_high)
    direct = total(own, from_down_low, from_down_high, from_up_low, from_up_high)

    source = mirror // ROWS
    position = source * SLOT + mirror % ROWS - pair * SLOT
    row = jnp.arange(ROWS, dtype=jnp.int32)
    pick = (position[:, None] == row[None, :]).astype(BF16)
    sends, lands = [], []
    for first, count in CHUNKS:
        slot = jnp.arange(count * V, dtype=jnp.int32)
        size = A_BLOCK * count
        step, core, second, inner = slot // (2 * size), slot // size % 2, slot % size // count, slot % count
        virt = (x + step) % NX * 2 + (c + core) % 2
        sends.append(((inner * V + virt * A_BLOCK + second)[:, None] == slot[None, :]).astype(BF16))
        virt = (x + NX - step) % NX * 2 + (c + core) % 2
        lands.append(((second * V + virt * A_BLOCK + first + inner)[:, None] == column[None, :]).astype(BF16))

    received = over_pair(direct[1])
    crossed = back(swap(turn(sends[0], direct[0])))
    begun = begin(lands[1], swap(turn(sends[1], received, pick)), direct)
    return finish(active, begun, pick, lands[0], over_pair(crossed))


def solution(mesh):
    grid = Mesh(mesh.devices.reshape(tuple(SIZE.values())), tuple(SIZE))
    rows, columns = ("z", "y"), ("x", "c")
    in_specs = (P(rows, columns), P(rows, None), P(rows, columns), P(rows))
    return jax.shard_map(local, mesh=grid, in_specs=in_specs, out_specs=P(rows, columns), check_vma=False)
```

```python
import jax
import jax.numpy as jnp
from jax import lax
from jax.experimental import pallas as pl
from jax.experimental.pallas import tpu as pltpu
from jax.sharding import Mesh, PartitionSpec as P

TW = 48
V = 96
SIZE = {"z": 8, "y": 4, "x": 4, "c": 2}
NZ, NY, NX = 8, 4, 4
VIRT = 8
PAIR = 32
A_BLOCK = V // VIRT
ROWS = 512
WIDTH = A_BLOCK * V
DEPTH = 288
SLOT = ROWS // PAIR
PLANE = NZ * SLOT
PIECE = A_BLOCK * A_BLOCK
HALF = ROWS // 2
CHUNKS = ((0, 8), (8, 4))
F32 = jnp.float32
BF16 = jnp.bfloat16
ROOM = pltpu.CompilerParams(vmem_limit_bytes=48 * 2**20)


def move(array, axis, by):
    n = SIZE[axis]
    return lax.ppermute(array, axis, [(i, (i + by) % n) for i in range(n)])


def product_kernel(outs_of, where_ref, *refs):
    blocks, b_ref, outs, a_ref = refs[:VIRT], refs[VIRT], refs[VIRT + 1:-1], refs[-1]
    for k, block in enumerate(blocks):
        a_ref[pl.ds(pl.multiple_of(where_ref[k] * DEPTH, 16), DEPTH), :] = block[0]
    value = lax.dot_general(a_ref[...], b_ref[...], (((0,), (0,)), ((), ())), preferred_element_type=F32)
    for g in range(len(outs) // outs_of):
        @pl.when(pl.program_id(0) == g)
        def _():
            rows = ROWS // outs_of
            for h in range(outs_of):
                out = outs[g * outs_of + h]
                out[...] = value[h * rows:(h + 1) * rows, :].astype(out.dtype)


def product(where, group, count, blocks, b, outs_of, kind, *first):
    shape = (ROWS // outs_of, WIDTH)
    whole = pl.BlockSpec((1, DEPTH, ROWS), lambda g, w: (group + g, 0, 0))
    part = pl.BlockSpec((1, DEPTH, ROWS), lambda g, w: (group % (NY // 2) + g, 0, 0))

    def kernel(*refs):
        product_kernel(outs_of, *refs[:VIRT + 2], *refs[VIRT + 2 + len(first):])

    return pl.pallas_call(
        kernel,
        grid_spec=pltpu.PrefetchScalarGridSpec(
            num_scalar_prefetch=1,
            grid=(count,),
            in_specs=[whole] * (VIRT - 2) + [part] * 2 + [pl.BlockSpec((VIRT * DEPTH, WIDTH), lambda g, w: (0, 0))]
            + [pl.BlockSpec(memory_space=pl.ANY)] * len(first),
            out_specs=[pl.BlockSpec(shape, lambda g, w: (0, 0))] * (count * outs_of),
            scratch_shapes=[pltpu.VMEM((VIRT * DEPTH, ROWS), BF16)],
        ),
        out_shape=[jax.ShapeDtypeStruct(shape, kind)] * (count * outs_of),
        compiler_params=ROOM,
    )(where, *blocks, b, *first)


def gather_x(block):
    half = NY // 2
    left = move(block, "x", 1)
    right = move(block, "x", -1)
    far_low = move(left[:half], "x", 1)
    far_high = move(right[half:], "x", -1)
    return [b for one in (block, left, right, far_low, far_high) for b in (one, move(one, "c", 1))]


def combine_kernel(up_ref, down_ref, from_down_ref, from_up_ref, *outs):
    first = pl.program_id(0) == 0
    up = (up_ref[...].astype(F32) + jnp.where(first, from_down_ref[...].astype(F32), 0)).astype(BF16)
    down = (down_ref[...].astype(F32) + jnp.where(first, 0, from_up_ref[...].astype(F32))).astype(BF16)
    for n, (at, count) in enumerate(CHUNKS):
        outs[2 * n][...] = up[:, at * V:(at + count) * V]
        outs[2 * n + 1][...] = down[:, at * V:(at + count) * V]


def combine(up, down, from_down, from_up):
    fixed = pl.BlockSpec((HALF, WIDTH), lambda i: (0, 0))
    moving = pl.BlockSpec((HALF, WIDTH), lambda i: (i, 0))
    widths = [count * V for _, count in CHUNKS for _ in range(2)]
    return pl.pallas_call(
        combine_kernel,
        grid=(2,),
        in_specs=[moving] * 2 + [fixed] * 2,
        out_specs=[pl.BlockSpec((HALF, w), lambda i: (i, 0)) for w in widths],
        out_shape=[jax.ShapeDtypeStruct((ROWS, w), BF16) for w in widths],
        compiler_params=ROOM,
    )(up, down, from_down, from_up)


def total_kernel(at, own_ref, down_ref, up_ref, out_ref):
    out_ref[...] = (own_ref[:, at] + down_ref[...].astype(F32) + up_ref[...].astype(F32)).astype(BF16)


def total(at, own, got_down, got_up):
    vmem = pl.BlockSpec(memory_space=pltpu.VMEM)

    def kernel(*refs):
        total_kernel(at, *refs)

    return pl.pallas_call(
        kernel,
        in_specs=[vmem] * 3,
        out_specs=vmem,
        out_shape=jax.ShapeDtypeStruct((ROWS, at.stop - at.start), BF16),
        compiler_params=ROOM,
    )(own, got_down, got_up)


def turn_kernel(send_ref, *refs):
    outs, rows = refs[-NX:], refs[0][...]
    if len(refs) == NX + 2:
        rows = jnp.dot(refs[1][...], rows, preferred_element_type=F32).astype(BF16)
    turned = lax.dot_general(send_ref[...], rows, (((1,), (1,)), ((), ())), preferred_element_type=F32).astype(BF16)
    size = turned.shape[0] // VIRT
    for d, out in enumerate(outs):
        for core in range(2):
            out[core] = turned[(2 * d + core) * size:(2 * d + core + 1) * size, :]


def turn(send, rows, *pick):
    vmem = pl.BlockSpec(memory_space=pltpu.VMEM)
    return pl.pallas_call(
        turn_kernel,
        in_specs=[vmem] * (2 + len(pick)),
        out_specs=[vmem] * NX,
        out_shape=[jax.ShapeDtypeStruct((2, send.shape[0] // VIRT, ROWS), BF16)] * NX,
        compiler_params=ROOM,
    )(send, rows, *pick)


def swap(sent):
    arrived = [sent[0]] + [move(sent[d], "x", d) for d in range(1, NX)]
    return arrived + [move(jnp.concatenate([block[1:] for block in arrived], axis=0), "c", 1)]


def stacked(blocks, u_ref):
    size = u_ref.shape[0] // VIRT
    for k in range(NX):
        u_ref[2 * k * size:(2 * k + 1) * size, :] = blocks[k][0]
        u_ref[(2 * k + 1) * size:(2 * k + 2) * size, :] = blocks[NX][k]


def back_kernel(*refs):
    stacked(refs[:NX + 1], refs[-1])
    refs[NX + 1][...] = refs[-1][...].T


def back(blocks):
    vmem = pl.BlockSpec(memory_space=pltpu.VMEM)
    width = VIRT * blocks[0].shape[1]
    return pl.pallas_call(
        back_kernel,
        in_specs=[vmem] * (1 + NX),
        out_specs=vmem,
        out_shape=jax.ShapeDtypeStruct((ROWS, width), BF16),
        scratch_shapes=[pltpu.VMEM((width, ROWS), BF16)],
        compiler_params=ROOM,
    )(*blocks)


def begin_kernel(land_ref, *refs):
    blocks, direct, o_ref, u_ref = refs[:NX + 1], refs[NX + 1:-2], refs[-2], refs[-1]
    stacked(blocks, u_ref)
    o_ref[...] = lax.dot_general(u_ref[...], land_ref[...], (((0,), (0,)), ((), ())), preferred_element_type=F32)
    for (first, count), part in zip(CHUNKS, direct):
        at = slice(first * V, (first + count) * V)
        o_ref[:, at] = o_ref[:, at] + part[...].astype(F32)


def begin(land, blocks, direct):
    vmem = pl.BlockSpec(memory_space=pltpu.VMEM)
    return pl.pallas_call(
        begin_kernel,
        in_specs=[vmem] * (2 + NX + len(direct)),
        out_specs=vmem,
        out_shape=jax.ShapeDtypeStruct((ROWS, WIDTH), F32),
        scratch_shapes=[pltpu.VMEM((land.shape[0], ROWS), BF16)],
        compiler_params=ROOM,
    )(land, *blocks, *direct)


def finish_kernel(active_ref, begun_ref, pick_ref, land_ref, received_ref, o_ref):
    picked = jnp.dot(pick_ref[...], received_ref[...], preferred_element_type=F32).astype(BF16)
    value = begun_ref[...] + jnp.dot(picked, land_ref[...], preferred_element_type=F32)
    column = lax.broadcasted_iota(jnp.int32, (ROWS, WIDTH), 1)
    live = jnp.where(lax.rem(column, V) < TW, active_ref[:, :1], active_ref[:, 1:]) > 0
    o_ref[...] = jnp.where(live, value, 0).astype(BF16)


def finish(active, begun, pick, land, received):
    vmem = pl.BlockSpec(memory_space=pltpu.VMEM)
    return pl.pallas_call(
        finish_kernel,
        in_specs=[vmem] * 5,
        out_specs=vmem,
        out_shape=jax.ShapeDtypeStruct((ROWS, WIDTH), BF16),
        compiler_params=ROOM,
    )(active, begun, pick, land, received)


def over_pair(rows):
    width = rows.shape[1]
    moved = lax.all_to_all(rows.reshape(PAIR, SLOT, width), ("z", "y"), split_axis=0, concat_axis=0, tiled=True)
    return moved.reshape(ROWS, width)


def local(amplitudes, block_mask, integrals, mirror):
    z, y, x, c = (lax.axis_index(n) for n in "zyxc")
    pair = z * NY + y
    tile = (x * 2 + c) * A_BLOCK // TW
    active = lax.dynamic_slice(block_mask, (0, 2 * tile), (ROWS, 2))
    column = jnp.arange(WIDTH, dtype=jnp.int32)
    live = jnp.where(((column % V) < TW)[None, :], active[:, :1], active[:, 1:]) > 0

    whole = lax.all_gather(integrals, "z", axis=0, tiled=True)

    masked = jnp.where(live, amplitudes, jnp.zeros_like(amplitudes))
    turned = masked.T.reshape(NY, DEPTH, ROWS)

    def toward(d):
        return lax.dynamic_slice_in_dim(turned, (y + d) % NY, 1, axis=0)

    groups = [toward(0), move(toward(2), "y", 2), move(toward(-1), "y", -1), move(toward(1), "y", 1)]
    blocks = gather_x(jnp.concatenate(groups, axis=0))
    low, high = blocks[:VIRT], blocks[:VIRT - 2] + blocks[VIRT:]
    where = jnp.stack([(x + d) % NX * 2 + core for d in (0, -1, 1, 2) for core in (c, 1 - c)]).astype(jnp.int32)

    far_low, far_high = product(where, 1, 1, low, whole, 2, BF16)
    from_down = move(far_low, "y", 1)
    from_up = move(far_high, "y", -1)
    up, down = product(where, 2, 2, high, whole, 1, BF16, far_low)
    up_last, down_last, up_first, down_first = combine(up, down, from_down, from_up)
    first = move(up_first, "y", 1), move(down_first, "y", -1)
    last = move(up_last, "y", 1), move(down_last, "y", -1)
    own, = product(where, 0, 1, low, whole, 1, F32, up_first)
    parts = [slice(first * V, (first + count) * V) for first, count in CHUNKS]
    direct = [total(parts[0], own, *last), total(parts[1], own, *first)]

    source = mirror // ROWS
    position = source * SLOT + mirror % ROWS - pair * SLOT
    row = jnp.arange(ROWS, dtype=jnp.int32)
    pick = (position[:, None] == row[None, :]).astype(BF16)
    sends, lands = [], []
    for first, count in CHUNKS:
        slot = jnp.arange(count * V, dtype=jnp.int32)
        size = A_BLOCK * count
        step, core, second, inner = slot // (2 * size), slot // size % 2, slot % size // count, slot % count
        virt = (x + step) % NX * 2 + (c + core) % 2
        sends.append(((inner * V + virt * A_BLOCK + second)[:, None] == slot[None, :]).astype(BF16))
        virt = (x + NX - step) % NX * 2 + (c + core) % 2
        lands.append(((second * V + virt * A_BLOCK + first + inner)[:, None] == column[None, :]).astype(BF16))

    received = over_pair(direct[1])
    crossed = back(swap(turn(sends[0], direct[0])))
    begun = begin(lands[1], swap(turn(sends[1], received, pick)), direct)
    return finish(active, begun, pick, lands[0], over_pair(crossed))


def solution(mesh):
    grid = Mesh(mesh.devices.reshape(tuple(SIZE.values())), tuple(SIZE))
    rows, columns = ("z", "y"), ("x", "c")
    in_specs = (P(rows, columns), P(rows, None), P(rows, columns), P(rows))
    return jax.shard_map(local, mesh=grid, in_specs=in_specs, out_specs=P(rows, columns), check_vma=False)
```
